32 devices in a mesh: grp: 2 (over x), lon: 16 (over z, y, core).
Axes of the slice: x: 2, y: 2, z: 4, core: 2. Of those that a mesh axis runs over, the one named last changes fastest.
Arguments:
- trajectory: bfloat16 [1280, 4, 4, 8, 192], P(('grp', 'lon')), parts along dimension 0, may hold values from -6 to 6
- lat_order: int32 [640], replicated, may hold values from 0 to 639, each once
- basis: float32 [8, 8, 192, 640], P('grp', None, 'lon'), parts along dimension 0, may hold values from -80 to 80, as said below
- weight: float32 [8, 640], replicated, may hold values from 0.3 to 3
Outputs:
- next_vector: float32 [16, 192, 640], P('grp', 'lon'), parts along dimension 0
- coefficients: float32 [10], P('grp'), parts along dimension 0
The draws below stay inside these ranges and needn't reach their ends.
There are 2 independent parts, one for each index of `grp`. The reference program is written for one: setup_inputs(seed, part) draws one part's arguments, and reference() takes and returns one part's arrays. A program takes and returns all parts, laid end to end along the dimension named above; an argument that names none is the same for every part. Nothing has to cross between parts.
Inputs may be any that keep to these rules, and one draw needn't show every extreme that they name: `basis`: lanczos vectors of earlier iterations, not orthogonal.
All inputs are finite; a program needn't handle non-finite values.
Results may differ from the reference program's by a relative error of at most 0.0008.
Values may be sent and summed in bfloat16 or wider, within the bound.
A program may use at most 192 MiB of HBM per device.

```python
import math
import jax
import jax.numpy as jnp
from jax import lax

LEV = 8
NLAT = 640
STEPS = 4
K = 4
NLON = 192


def draw_basis(key, part):
    key = jax.random.fold_in(key, 11)
    first, second = jax.random.split(key, 2)
    lon_pos = jnp.arange(NLON, dtype=jnp.float32)[None, None, :, None]
    lon_scale = 3.0 ** (lon_pos / NLON)
    own = jnp.clip(jax.random.normal(first, (K, LEV, NLON, NLAT), jnp.float32), -6.0, 6.0)
    common = jnp.clip(jax.random.normal(second, (1, LEV, NLON, NLAT), jnp.float32), -6.0, 6.0)
    return (0.7 * common + 0.7 * own) * lon_scale


def block_levels(own_key, shape, shards, low, top_value):
    gain = 1.0
    for axis_at, blocks in shards:
        heights = jax.random.uniform(jax.random.fold_in(jax.random.fold_in(own_key, 6), axis_at), (blocks,), jnp.float32, low / len(shards), top_value / len(shards))
        gain = gain * jnp.repeat(jnp.exp(heights), shape[axis_at] // blocks).reshape((-1,) + (1,) * (len(shape) - 1 - axis_at))
    return gain


def bell_draw(own_key, extent, scale, most, cuts=(), kind=jnp.bfloat16):
    entries = scale * jax.random.normal(own_key, extent, jnp.float32)
    if cuts:
        entries = entries * block_levels(own_key, extent, cuts, -0.22, 0.18)
    return jnp.clip(entries, -most, most).astype(kind)


def setup_inputs(seed: int = 0, part: int = 0) -> dict:
    arg_keys = jax.random.split(jax.random.key(seed), 5)
    part_keys = jax.random.split(jax.random.fold_in(arg_keys[4], part), 5)
    return {
        "trajectory": bell_draw(part_keys[0], (NLAT, STEPS, 4, LEV, NLON), 1.0, 6.0, ((0, 16),)),
        "lat_order": jax.random.permutation(arg_keys[1], NLAT).astype(jnp.int32),
        "basis": draw_basis(jax.random.fold_in(jax.random.fold_in(arg_keys[4], part), 71), part),
        "weight": jnp.clip(jnp.exp(jax.random.uniform(arg_keys[3], (LEV, NLAT), jnp.float32, math.log(0.3), math.log(3.0))), 0.3, 3.0),
    }


def north(f):
    return jnp.concatenate([f[:, :, 1:], jnp.zeros_like(f[:, :, :1])], axis=2)

def south(f):
    return jnp.concatenate([jnp.zeros_like(f[:, :, :1]), f[:, :, :-1]], axis=2)

def upper(f):
    return jnp.concatenate([f[1:], jnp.zeros_like(f[:1])], axis=0)

def lower(f):
    return jnp.concatenate([jnp.zeros_like(f[:1]), f[:-1]], axis=0)

def make_fields(raw):
    return (0.2 * jnp.tanh(raw[0]), 0.2 * jnp.tanh(raw[1]), 0.04 + 0.11 * jax.nn.sigmoid(raw[2]), 0.02 + 0.08 * jax.nn.sigmoid(raw[3]))

def tl_step(x, fields):
    u, v, k, m = fields
    east = jnp.roll(x, -1, axis=1)
    west = jnp.roll(x, 1, axis=1)
    nn = north(x)
    ss = south(x)
    return x - 0.5 * u * (east - west) - 0.5 * v * (nn - ss) + k * (east + west + nn + ss - 4.0 * x) + m * (upper(x) + lower(x) - 2.0 * x)

def adjoint_step(y, fields):
    u, v, k, m = fields
    flux_u = u * y
    flux_v = v * y
    flux_k = k * y
    flux_m = m * y
    east_u = jnp.roll(flux_u, -1, axis=1)
    west_u = jnp.roll(flux_u, 1, axis=1)
    east_k = jnp.roll(flux_k, -1, axis=1)
    west_k = jnp.roll(flux_k, 1, axis=1)
    return y + 0.5 * (east_u - west_u) + 0.5 * (north(flux_v) - south(flux_v)) + (east_k + west_k + north(flux_k) + south(flux_k) - 4.0 * flux_k) + (upper(flux_m) + lower(flux_m) - 2.0 * flux_m)

def reference(trajectory, lat_order, basis, weight):
    inverse = jnp.argsort(lat_order).astype(jnp.int32)
    natural = jnp.take(trajectory, inverse, axis=0).astype(jnp.float32)
    natural = jnp.transpose(natural, (1, 2, 3, 4, 0))
    steps_count = natural.shape[0]
    kept = basis.shape[0]
    state = basis[kept - 1]
    for step in range(steps_count):
        state = tl_step(state, make_fields(natural[step]))
    state = weight[:, None, :] * state
    for step in range(steps_count - 1, -1, -1):
        state = adjoint_step(state, make_fields(natural[step]))
    projections = lax.optimization_barrier(jnp.mean(basis * state[None], axis=(1, 2, 3)))
    resid = state - jnp.tensordot(projections, basis, axes=1, precision=jax.lax.Precision.HIGHEST)
    beta = jnp.sqrt(jnp.mean(resid * resid) + 1e-06)
    return (resid / beta, jnp.concatenate([projections, beta[None]]))
```

```python
import functools

import jax
import jax.numpy as jnp
from jax import lax
from jax.experimental import pallas as pl
from jax.experimental.pallas import tpu as pltpu
from jax.sharding import PartitionSpec as P

BF16 = jnp.bfloat16
F32 = jnp.float32
VMEM = pl.BlockSpec(memory_space=pltpu.VMEM)
MIB = 1024 * 1024


def pairs(kept):
    return [(a, b) for a in range(kept) for b in range(a, kept)]


def pack_kernel(rows, t_ref, out_ref, wide):
    lons = t_ref.shape[2]
    eye = (
        lax.broadcasted_iota(jnp.int32, (lons, lons), 0)
        == lax.broadcasted_iota(jnp.int32, (lons, lons), 1)
    ).astype(F32).astype(BF16)
    for r in range(rows):
        turned = lax.dot_general(
            eye, t_ref[r], (((1,), (1,)), ((), ())), preferred_element_type=F32
        )
        wide[pl.ds(r, lons, stride=rows), :] = turned
    out_ref[...] = wide[...].astype(BF16)


def row_sum(cells):
    total = jnp.sum(jnp.sum(cells, axis=0), axis=0, keepdims=True)
    return sum(total[:, at : at + 128] for at in range(0, total.shape[1], 128))


def prep_kernel(lat_ref, basis_ref, perm_ref, gram_ref):
    lats = perm_ref.shape[0]
    kept = basis_ref.shape[0]
    perm_ref[...] = (
        (lat_ref[...] == lax.broadcasted_iota(jnp.int32, (lats, lats), 1))
        .astype(F32)
        .astype(BF16)
    )
    gram_ref[...] = jnp.zeros_like(gram_ref)
    for at, (a, b) in enumerate(pairs(kept)):
        gram_ref[kept + 1 + at : kept + 2 + at, :] = row_sum(basis_ref[a] * basis_ref[b])


def main_kernel(
    count, rows, cells, recv_ref, perm_ref, basis_ref, weight_ref, gram_ref,
    out_ref, coef_ref,
    wide, coefs, state, halo, edge, gathered,
    halo_send, halo_recv, sum_send, sum_recv,
):
    kept, tile, levels, lats = basis_ref.shape
    steps = coefs.shape[0]
    me = lax.axis_index("lon")
    west = lax.rem(me + count - 1, count)
    east = lax.rem(me + 1, count)
    barrier = pltpu.get_barrier_semaphore()

    @pl.loop(1, count)
    def _(d):
        pl.semaphore_signal(
            barrier, inc=1, device_id={"lon": lax.rem(me + d, count)},
            device_id_type=pl.DeviceIdType.MESH,
        )

    wide[...] = recv_ref[...].astype(F32)
    level = lax.broadcasted_iota(jnp.int32, (levels, lats), 0)
    lat = lax.broadcasted_iota(jnp.int32, (levels, lats), 1)
    up = (level < levels - 1).astype(F32)
    down = (level > 0).astype(F32)
    not_north = (lat < lats - 1).astype(F32)
    not_south = (lat > 0).astype(F32)

    def fields(i, _):
        block = wide[:, pl.ds(pl.multiple_of(i * rows, 8), rows), :]
        block = block.reshape(lats, block.shape[2]).astype(BF16)
        raw = lax.dot_general(
            block, perm_ref[...], (((0,), (0,)), ((), ())), preferred_element_type=F32
        ).reshape(steps, 4, levels, lats)
        u = 0.1 * jnp.tanh(raw[:, 0])
        v = 0.1 * jnp.tanh(raw[:, 1])
        k = 0.095 + 0.055 * jnp.tanh(0.5 * raw[:, 2])
        m = 0.06 + 0.04 * jnp.tanh(0.5 * raw[:, 3])
        coefs[:, 0, i] = 1.0 - 4.0 * k - 2.0 * m
        coefs[:, 1, i] = k - u
        coefs[:, 2, i] = k + u
        coefs[:, 3, i] = (k - v) * not_north
        coefs[:, 4, i] = (k + v) * not_south
        coefs[:, 5, i] = m
        return 0

    def copies(slot):
        return [
            pltpu.make_async_remote_copy(
                src_ref=edge.at[slot, side],
                dst_ref=halo.at[slot, side],
                send_sem=halo_send.at[slot, side],
                recv_sem=halo_recv.at[slot, side],
                device_id={"lon": peer},
                device_id_type=pl.DeviceIdType.MESH,
            )
            for side, peer in ((0, west), (1, east))
        ]

    def send(slot, first, last):
        edge[slot, 0] = first
        edge[slot, 1] = last
        for copy in copies(slot):
            copy.start()

    def receive(slot):
        for copy in copies(slot):
            copy.wait_recv()
        return halo[slot, 0][None], halo[slot, 1][None]

    def roll(x, by, axis):
        shape = x.shape
        if axis == 2:
            return pltpu.roll(x.reshape(-1, lats), by % lats, 1).reshape(shape)
        return pltpu.roll(x, by % levels, 1)

    def forward(s, lo, hi, x, xe, xw):
        c = lambda at: coefs[s, at, lo:hi]
        return (
            c(0) * x
            + c(1) * xe
            + c(2) * xw
            + c(3) * roll(x, -1, 2)
            + c(4) * roll(x, 1, 2)
            + c(5) * (up * roll(x, -1, 1) + down * roll(x, 1, 1))
        )

    def adjoint(s, lo, hi, y, fe, fw):
        c = lambda at: coefs[s, at, lo:hi]
        d = c(5) * y
        return (
            c(0) * y
            + fe
            + fw
            + roll(c(4) * y, -1, 2)
            + roll(c(3) * y, 1, 2)
            + roll(down * d, -1, 1)
            + roll(up * d, 1, 1)
        )

    half = tile // 2
    lax.fori_loop(0, half, fields, 0)
    pl.semaphore_wait(barrier, count - 1)
    state[0] = basis_ref[kept - 1]
    send(0, state[0, 0], state[0, tile - 1])
    lax.fori_loop(half, tile, fields, 0)

    for t in range(2 * steps):
        now, new = t % 2, (t + 1) % 2
        if t < steps:
            s = t
            inside = forward(
                s, 1, tile - 1, state[now, 1 : tile - 1],
                state[now, 2:tile], state[now, 0 : tile - 2],
            )
            he, hw = receive(t)
            first = forward(s, 0, 1, state[now, 0:1], state[now, 1:2], hw)
            last = forward(
                s, tile - 1, tile, state[now, tile - 1 : tile], he,
                state[now, tile - 2 : tile - 1],
            )
            if t == steps - 1:
                inside = weight_ref[...] * inside
                first = weight_ref[...] * first
                last = weight_ref[...] * last
        else:
            s = 2 * steps - 1 - t
            inside = adjoint(
                s, 1, tile - 1, state[now, 1 : tile - 1],
                coefs[s, 2, 2:tile] * state[now, 2:tile],
                coefs[s, 1, 0 : tile - 2] * state[now, 0 : tile - 2],
            )
            he, hw = receive(t)
            first = adjoint(
                s, 0, 1, state[now, 0:1], coefs[s, 2, 1:2] * state[now, 1:2], hw
            )
            last = adjoint(
                s, tile - 1, tile, state[now, tile - 1 : tile], he,
                coefs[s, 1, tile - 2 : tile - 1] * state[now, tile - 2 : tile - 1],
            )
        if t < steps - 1:
            send(t + 1, first[0], last[0])
        elif t < 2 * steps - 1:
            s = 2 * steps - 2 - t
            send(t + 1, coefs[s, 2, 0] * first[0], coefs[s, 1, tile - 1] * last[0])
        state[new, 0:1] = first
        state[new, tile - 1 : tile] = last
        state[new, 1 : tile - 1] = inside

    w = state[0]
    own = [row_sum(basis_ref[k] * w) for k in range(kept)] + [row_sum(w * w)]
    gathered[me] = gram_ref[...]
    for k in range(kept + 1):
        gathered[me, k : k + 1, :] = own[k]

    def share(d):
        return pltpu.make_async_remote_copy(
            src_ref=gathered.at[me],
            dst_ref=gathered.at[me],
            send_sem=sum_send.at[d],
            recv_sem=sum_recv.at[me],
            device_id={"lon": lax.rem(me + d, count)},
            device_id_type=pl.DeviceIdType.MESH,
        )

    @pl.loop(1, count)
    def _(d):
        share(d).start()

    @pl.loop(1, count)
    def _(d):
        source = lax.rem(me + d, count)
        pltpu.make_async_remote_copy(
            src_ref=gathered.at[source],
            dst_ref=gathered.at[source],
            send_sem=sum_send.at[d],
            recv_sem=sum_recv.at[source],
            device_id={"lon": source},
            device_id_type=pl.DeviceIdType.MESH,
        ).wait_recv()

    total = jnp.sum(jnp.sum(gathered[...], axis=0), axis=1, keepdims=True) / cells
    c = [total[k : k + 1] for k in range(kept)]
    square = total[kept : kept + 1] - 2.0 * sum(x * x for x in c)
    for at, (a, b) in enumerate(pairs(kept)):
        g = total[kept + 1 + at : kept + 2 + at]
        square = square + (1.0 if a == b else 2.0) * c[a] * c[b] * g
    beta = jnp.sqrt(square + 1e-06)
    for k in range(kept):
        coef_ref[k : k + 1, :] = jnp.broadcast_to(c[k], (1, 128))
    coef_ref[kept : kept + 1, :] = jnp.broadcast_to(beta, (1, 128))
    coef_ref[kept + 1 :, :] = jnp.zeros((8 - kept - 1, 128), F32)
    scale = jnp.broadcast_to(1.0 / beta, (levels, lats))
    full = [jnp.broadcast_to(x, (levels, lats)) for x in c]
    for i in range(tile):
        r = state[0, i]
        for k in range(kept):
            r = r - full[k] * basis_ref[k, i]
        out_ref[i] = r * scale

    for t in range(2 * steps):
        for copy in copies(t):
            copy.wait_send()

    @pl.loop(1, count)
    def _(d):
        share(d).wait_send()


def shards(trajectory, lat_order, basis, weight):
    rows, steps, states, levels, lons = trajectory.shape
    kept, _, tile, lats = basis.shape
    count = lax.axis_size("lon")
    lanes = steps * states * levels
    cells = float(levels * lons * lats)
    flat = trajectory.reshape(rows, lanes, lons)
    if rows % 8 == 0:
        packed = pl.pallas_call(
            functools.partial(pack_kernel, rows),
            out_shape=jax.ShapeDtypeStruct((lons * rows, lanes), BF16),
            in_specs=[VMEM],
            out_specs=VMEM,
            scratch_shapes=[pltpu.VMEM((lons * rows, lanes), F32)],
            compiler_params=pltpu.CompilerParams(vmem_limit_bytes=24 * MIB),
            name="pack",
        )(flat)
    else:
        packed = jnp.transpose(flat, (2, 0, 1))
    received = lax.all_to_all(
        packed.reshape(count, tile * rows, lanes), "lon", split_axis=0, concat_axis=0, tiled=True
    )
    if rows % 8:
        received = jnp.transpose(received.reshape(count, tile, rows, lanes), (1, 0, 2, 3))
        received = received.reshape(1, tile * lats, lanes)
        rows = lats
    turned = jnp.transpose(basis, (0, 2, 1, 3))
    perm, gram = pl.pallas_call(
        prep_kernel,
        out_shape=(
            jax.ShapeDtypeStruct((lats, lats), BF16),
            jax.ShapeDtypeStruct((16, 128), F32),
        ),
        in_specs=[VMEM] * 2,
        out_specs=(VMEM, VMEM),
        cost_estimate=pl.CostEstimate(
            flops=20_000_000, bytes_accessed=4_000_000, transcendentals=0
        ),
        compiler_params=pltpu.CompilerParams(vmem_limit_bytes=16 * MIB),
        name="prepare",
    )(lat_order[:, None], turned)
    slots = 2 * steps
    out, coef = pl.pallas_call(
        functools.partial(main_kernel, count, rows, cells),
        out_shape=(
            jax.ShapeDtypeStruct((tile, levels, lats), F32),
            jax.ShapeDtypeStruct((8, 128), F32),
        ),
        in_specs=[VMEM] * 5,
        out_specs=(VMEM, VMEM),
        scratch_shapes=[
            pltpu.VMEM(received.shape, F32),
            pltpu.VMEM((steps, 6, tile, levels, lats), F32),
            pltpu.VMEM((2, tile, levels, lats), F32),
            pltpu.VMEM((slots, 2, levels, lats), F32),
            pltpu.VMEM((slots, 2, levels, lats), F32),
            pltpu.VMEM((count, 16, 128), F32),
            pltpu.SemaphoreType.DMA((slots, 2)),
            pltpu.SemaphoreType.DMA((slots, 2)),
            pltpu.SemaphoreType.DMA((count,)),
            pltpu.SemaphoreType.DMA((count,)),
        ],
        compiler_params=pltpu.CompilerParams(
            collective_id=0, has_side_effects=True, vmem_limit_bytes=40 * MIB
        ),
        name="iterate",
    )(received, perm, turned, weight, gram)
    return jnp.transpose(out, (1, 0, 2)), coef[: kept + 1, 0]


def solution(mesh):
    placed = (P(("grp", "lon"), None, None, None, None), P(), P("grp", None, "lon", None), P())
    return jax.shard_map(
        shards,
        mesh=mesh,
        in_specs=placed,
        out_specs=(P("grp", "lon", None), P("grp")),
        check_vma=False,
    )
```

```python
import functools

import jax
import jax.numpy as jnp
from jax import lax
from jax.experimental import pallas as pl
from jax.experimental.pallas import tpu as pltpu
from jax.sharding import PartitionSpec as P

BF16 = jnp.bfloat16
F32 = jnp.float32
VMEM = pl.BlockSpec(memory_space=pltpu.VMEM)
MIB = 1024 * 1024


def pairs(kept):
    return [(a, b) for a in range(kept) for b in range(a, kept)]


def row_sum(cells):
    total = jnp.sum(jnp.sum(cells, axis=0), axis=0, keepdims=True)
    return sum(total[:, at : at + 128] for at in range(0, total.shape[1], 128))


def main_kernel(
    count, rows, cells, fused, source_ref, lat_ref, basis_hbm, weight_ref,
    out_ref, coef_ref,
    wide, coefs, state, halo, edge, gathered, perm, basis_ref,
    halo_send, halo_recv, sum_send, sum_recv, load_sem, *more,
):
    kept, tile, levels, lats = basis_ref.shape
    steps = coefs.shape[0]
    quads = tile // 4
    me = lax.axis_index("lon")
    west = lax.rem(me + count - 1, count)
    east = lax.rem(me + 1, count)
    barrier = pltpu.get_barrier_semaphore()

    @pl.loop(1, count)
    def _(d):
        pl.semaphore_signal(
            barrier, inc=1, device_id={"lon": lax.rem(me + d, count)},
            device_id_type=pl.DeviceIdType.MESH,
        )

    load_last = pltpu.make_async_copy(
        basis_hbm.at[kept - 1], basis_ref.at[kept - 1], load_sem.at[0]
    )
    load_rest = pltpu.make_async_copy(
        basis_hbm.at[0 : kept - 1], basis_ref.at[0 : kept - 1], load_sem.at[1]
    )
    level = lax.broadcasted_iota(jnp.int32, (levels, lats), 0)
    lat = lax.broadcasted_iota(jnp.int32, (levels, lats), 1)
    up = (level < levels - 1).astype(F32)
    down = (level > 0).astype(F32)
    not_north = (lat < lats - 1).astype(F32)
    not_south = (lat > 0).astype(F32)

    def fields(s):
        for quad in range(quads):
            at = (s * quads + quad) * rows
            block = wide[:, at : at + rows, :].reshape(lats, 128).astype(BF16)
            raw = lax.dot_general(
                block, perm[...], (((0,), (0,)), ((), ())), preferred_element_type=F32
            ).reshape(4, 4, levels, lats)
            u = 0.1 * jnp.tanh(raw[:, 0])
            v = 0.1 * jnp.tanh(raw[:, 1])
            k = 0.095 + 0.055 * jnp.tanh(0.5 * raw[:, 2])
            m = 0.06 + 0.04 * jnp.tanh(0.5 * raw[:, 3])
            cols = slice(4 * quad, 4 * quad + 4)
            coefs[s, 0, cols] = 1.0 - 4.0 * k - 2.0 * m
            coefs[s, 1, cols] = k - u
            coefs[s, 2, cols] = k + u
            coefs[s, 3, cols] = (k - v) * not_north
            coefs[s, 4, cols] = (k + v) * not_south
            coefs[s, 5, cols] = m

    def copies(slot):
        return [
            pltpu.make_async_remote_copy(
                src_ref=edge.at[slot, side],
                dst_ref=halo.at[slot, side],
                send_sem=halo_send.at[slot, side],
                recv_sem=halo_recv.at[slot, side],
                device_id={"lon": peer},
                device_id_type=pl.DeviceIdType.MESH,
            )
            for side, peer in ((0, west), (1, east))
        ]

    def send(slot, first, last):
        edge[slot, 0] = first
        edge[slot, 1] = last
        for copy in copies(slot):
            copy.start()

    def receive(slot):
        for copy in copies(slot):
            copy.wait_recv()
        return halo[slot, 0][None], halo[slot, 1][None]

    def roll(x, by, axis):
        shape = x.shape
        if axis == 2:
            return pltpu.roll(x.reshape(-1, lats), by % lats, 1).reshape(shape)
        return pltpu.roll(x, by % levels, 1)

    def forward(s, lo, hi, x, xe, xw):
        c = lambda at: coefs[s, at, lo:hi]
        return (
            c(0) * x
            + c(1) * xe
            + c(2) * xw
            + c(3) * roll(x, -1, 2)
            + c(4) * roll(x, 1, 2)
            + c(5) * (up * roll(x, -1, 1) + down * roll(x, 1, 1))
        )

    def adjoint(s, lo, hi, y, fe, fw):
        c = lambda at: coefs[s, at, lo:hi]
        d = c(5) * y
        return (
            c(0) * y
            + fe
            + fw
            + roll(c(4) * y, -1, 2)
            + roll(c(3) * y, 1, 2)
            + roll(down * d, -1, 1)
            + roll(up * d, 1, 1)
        )

    def prepare():
        perm[...] = jnp.transpose(
            (lax.broadcasted_iota(jnp.int32, (lats, lats), 0) == lat_ref[...]).astype(F32)
        ).astype(BF16)
        gathered[me] = jnp.zeros((16, 128), F32)
        for at, (a, b) in enumerate(pairs(kept)):
            gathered[me, kept + 1 + at : kept + 2 + at, :] = row_sum(basis_ref[a] * basis_ref[b])

    def start_state():
        load_last.wait()
        state[0] = basis_ref[kept - 1]
        send(0, state[0, 0], state[0, tile - 1])

    if fused:
        raw_ref, turned, outbox, inbox, raw_sem, box_send, box_recv = more
        lanes, lons = raw_ref.shape[2], raw_ref.shape[3]
        per_step = quads * rows
        bounds = [-(-s * per_step // 16) * 16 for s in range(steps + 1)]
        loads = [
            pltpu.make_async_copy(
                source_ref.at[:, s * lanes : (s + 1) * lanes], raw_ref.at[s], raw_sem.at[s]
            )
            for s in range(steps)
        ]
        loads[0].start()
        load_last.start()
        for load in loads[1:]:
            load.start()
        load_rest.start()
        row = lax.broadcasted_iota(jnp.int32, (4 * lanes, lons), 0)
        lon = lax.broadcasted_iota(jnp.int32, (4 * lanes, lons), 1)
        quarter = lon & 3
        keep = sum(
            ((row >= lanes * q) & (row < lanes * (q + 1)) & (quarter == q)).astype(F32)
            for q in range(4)
        ).astype(BF16)
        row = lax.broadcasted_iota(jnp.int32, (lons // 4, lons), 0)
        lon = lax.broadcasted_iota(jnp.int32, (lons // 4, lons), 1)
        pick = ((lon >= 4 * row) & (lon < 4 * row + 4)).astype(F32).astype(BF16)

        def turn(s, lo, hi):
            for r in range(lo, hi):
                a = raw_ref[s, r]
                a = jnp.concatenate([a, a, a, a], axis=0) * keep
                turned[pl.ds(s * count * per_step + r, lons // 4, stride=rows), :] = (
                    lax.dot_general(
                        pick, a, (((1,), (1,)), ((), ())), preferred_element_type=F32
                    )
                )

        def step_rows(s, lo, hi):
            whole = turned[s * count * per_step : (s + 1) * count * per_step]
            return whole.reshape(count, per_step, 128)[:, lo:hi]

        def pack(p):
            lo, hi = bounds[p], bounds[p + 1]
            parts = [step_rows(p, lo - p * per_step, per_step)]
            if hi > (p + 1) * per_step:
                parts.append(step_rows(p + 1, 0, hi - (p + 1) * per_step))
            outbox[:, lo:hi] = jnp.concatenate(parts, axis=1).astype(BF16)
            inbox[me, lo:hi] = outbox[me, lo:hi]

        def box(p, target, source, d):
            lo, hi = bounds[p], bounds[p + 1]
            return pltpu.make_async_remote_copy(
                src_ref=outbox.at[target, lo:hi],
                dst_ref=inbox.at[source, lo:hi],
                send_sem=box_send.at[p, d],
                recv_sem=box_recv.at[p, source],
                device_id={"lon": target},
                device_id_type=pl.DeviceIdType.MESH,
            )

        def post(p):
            @pl.loop(1, count)
            def _(d):
                box(p, lax.rem(me + d, count), me, d).start()

        def arrive(p):
            @pl.loop(1, count)
            def _(d):
                source = lax.rem(me + d, count)
                box(p, source, source, d).wait_recv()

            lo, hi = bounds[p], bounds[p + 1]
            wide[:, lo:hi] = inbox[:, lo:hi].astype(F32)

        loads[0].wait()
        turn(0, 0, rows)
        loads[1].wait()
        turn(1, 0, 8)
        pack(0)
        pl.semaphore_wait(barrier, count - 1)
        start_state()
        post(0)
        turn(1, 8, rows)
        pack(1)
        post(1)
        for s in range(2, steps):
            loads[s].wait()
            turn(s, 0, rows)
        for s in range(2, steps):
            pack(s)
        load_rest.wait()
        prepare()
    else:
        load_last.start()
        load_rest.start()
        wide[...] = source_ref[...].astype(F32)
        pl.semaphore_wait(barrier, count - 1)
        start_state()
        load_rest.wait()
        prepare()

    for t in range(2 * steps):
        now, new = t % 2, (t + 1) % 2
        if t < steps:
            s = t
            if fused:
                arrive(t)
            fields(t)
            inside = forward(
                s, 1, tile - 1, state[now, 1 : tile - 1],
                state[now, 2:tile], state[now, 0 : tile - 2],
            )
            he, hw = receive(t)
            first = forward(s, 0, 1, state[now, 0:1], state[now, 1:2], hw)
            last = forward(
                s, tile - 1, tile, state[now, tile - 1 : tile], he,
                state[now, tile - 2 : tile - 1],
            )
            if t == steps - 1:
                inside = weight_ref[...] * inside
                first = weight_ref[...] * first
                last = weight_ref[...] * last
        else:
            s = 2 * steps - 1 - t
            inside = adjoint(
                s, 1, tile - 1, state[now, 1 : tile - 1],
                coefs[s, 2, 2:tile] * state[now, 2:tile],
                coefs[s, 1, 0 : tile - 2] * state[now, 0 : tile - 2],
            )
            he, hw = receive(t)
            first = adjoint(
                s, 0, 1, state[now, 0:1], coefs[s, 2, 1:2] * state[now, 1:2], hw
            )
            last = adjoint(
                s, tile - 1, tile, state[now, tile - 1 : tile], he,
                coefs[s, 1, tile - 2 : tile - 1] * state[now, tile - 2 : tile - 1],
            )
        if t < steps - 1:
            send(t + 1, first[0], last[0])
        elif t < 2 * steps - 1:
            s = 2 * steps - 2 - t
            send(t + 1, coefs[s, 2, 0] * first[0], coefs[s, 1, tile - 1] * last[0])
        state[new, 0:1] = first
        state[new, tile - 1 : tile] = last
        state[new, 1 : tile - 1] = inside
        if fused and t + 2 < steps:
            post(t + 2)

    w = state[0]
    own = [row_sum(basis_ref[k] * w) for k in range(kept)] + [row_sum(w * w)]
    for k in range(kept + 1):
        gathered[me, k : k + 1, :] = own[k]

    def share(d):
        return pltpu.make_async_remote_copy(
            src_ref=gathered.at[me],
            dst_ref=gathered.at[me],
            send_sem=sum_send.at[d],
            recv_sem=sum_recv.at[me],
            device_id={"lon": lax.rem(me + d, count)},
            device_id_type=pl.DeviceIdType.MESH,
        )

    @pl.loop(1, count)
    def _(d):
        share(d).start()

    @pl.loop(1, count)
    def _(d):
        source = lax.rem(me + d, count)
        pltpu.make_async_remote_copy(
            src_ref=gathered.at[source],
            dst_ref=gathered.at[source],
            send_sem=sum_send.at[d],
            recv_sem=sum_recv.at[source],
            device_id={"lon": source},
            device_id_type=pl.DeviceIdType.MESH,
        ).wait_recv()

    total = jnp.sum(jnp.sum(gathered[...], axis=0), axis=1, keepdims=True) / cells
    c = [total[k : k + 1] for k in range(kept)]
    square = total[kept : kept + 1] - 2.0 * sum(x * x for x in c)
    for at, (a, b) in enumerate(pairs(kept)):
        g = total[kept + 1 + at : kept + 2 + at]
        square = square + (1.0 if a == b else 2.0) * c[a] * c[b] * g
    beta = jnp.sqrt(square + 1e-06)
    lane = lax.broadcasted_iota(jnp.int32, (8, 128), 1)
    coef_ref[...] = sum(
        jnp.where(lane == k, jnp.broadcast_to(x, (8, 128)), 0.0)
        for k, x in enumerate(c + [beta])
    )
    scale = jnp.broadcast_to(1.0 / beta, (levels, lats))
    full = [jnp.broadcast_to(x, (levels, lats)) for x in c]
    for i in range(tile):
        r = state[0, i]
        for k in range(kept):
            r = r - full[k] * basis_ref[k, i]
        out_ref[i] = r * scale

    for t in range(2 * steps):
        for copy in copies(t):
            copy.wait_send()

    @pl.loop(1, count)
    def _(d):
        share(d).wait_send()

    if fused:
        for p in range(steps):

            @pl.loop(1, count)
            def _(d, p=p):
                box(p, lax.rem(me + d, count), me, d).wait_send()


def shards(trajectory, lat_order, basis, weight):
    rows, steps, states, levels, lons = trajectory.shape
    kept, _, tile, lats = basis.shape
    count = lax.axis_size("lon")
    lanes = steps * states * levels
    cells = float(levels * lons * lats)
    flat = trajectory.reshape(rows, lanes, lons)
    quads = tile // 4
    fused = rows % 8 == 0 and (steps * quads * rows) % 16 == 0 and steps % 2 == 0
    slots = 2 * steps
    more = []
    if fused:
        source, place, blocks, run = flat, pl.BlockSpec(memory_space=pl.ANY), count, rows
        more = [
            pltpu.VMEM((steps, rows, lanes // steps, lons), BF16),
            pltpu.VMEM((lons * rows, lanes), F32),
            pltpu.VMEM((count, tile * rows, lanes), BF16),
            pltpu.VMEM((count, tile * rows, lanes), BF16),
            pltpu.SemaphoreType.DMA((steps,)),
            pltpu.SemaphoreType.DMA((steps, count)),
            pltpu.SemaphoreType.DMA((steps, count)),
        ]
    else:
        packed = jnp.transpose(flat, (2, 0, 1)).reshape(count, tile * rows, lanes)
        got = lax.all_to_all(packed, "lon", split_axis=0, concat_axis=0, tiled=True)
        got = got.reshape(count, quads, 4, rows, steps, lanes // steps)
        got = jnp.transpose(got, (4, 1, 0, 3, 2, 5))
        source, place, blocks, run = got.reshape(1, tile * lats, lanes), VMEM, 1, lats
    out, coef = pl.pallas_call(
        functools.partial(main_kernel, count, run, cells, fused),
        out_shape=(
            jax.ShapeDtypeStruct((tile, levels, lats), F32),
            jax.ShapeDtypeStruct((8, 128), F32),
        ),
        in_specs=[place, VMEM, pl.BlockSpec(memory_space=pl.ANY), VMEM],
        out_specs=(VMEM, VMEM),
        scratch_shapes=[
            pltpu.VMEM((blocks, tile * run, lanes), F32),
            pltpu.VMEM((steps, 6, tile, levels, lats), F32),
            pltpu.VMEM((2, tile, levels, lats), F32),
            pltpu.VMEM((slots, 2, levels, lats), F32),
            pltpu.VMEM((slots, 2, levels, lats), F32),
            pltpu.VMEM((count, 16, 128), F32),
            pltpu.VMEM((lats, lats), BF16),
            pltpu.VMEM((kept, tile, levels, lats), F32),
            pltpu.SemaphoreType.DMA((slots, 2)),
            pltpu.SemaphoreType.DMA((slots, 2)),
            pltpu.SemaphoreType.DMA((count,)),
            pltpu.SemaphoreType.DMA((count,)),
            pltpu.SemaphoreType.DMA((2,)),
        ]
        + more,
        compiler_params=pltpu.CompilerParams(
            collective_id=0, has_side_effects=True, vmem_limit_bytes=63 * MIB
        ),
        name="iterate",
    )(source, lat_order[None], jnp.transpose(basis, (0, 2, 1, 3)), weight)
    return jnp.transpose(out, (1, 0, 2)), coef[0, : kept + 1]


def solution(mesh):
    placed = (P(("grp", "lon"), None, None, None, None), P(), P("grp", None, "lon", None), P())
    return jax.shard_map(
        shards,
        mesh=mesh,
        in_specs=placed,
        out_specs=(P("grp", "lon", None), P("grp")),
        check_vma=False,
    )
```

```python
import functools

import jax
import jax.numpy as jnp
from jax import lax
from jax.experimental import pallas as pl
from jax.experimental.pallas import tpu as pltpu
from jax.sharding import PartitionSpec as P

BF16 = jnp.bfloat16
F32 = jnp.float32
VMEM = pl.BlockSpec(memory_space=pltpu.VMEM)
MIB = 1024 * 1024


def pairs(kept):
    return [(a, b) for a in range(kept) for b in range(a, kept)]


def row_sum(cells):
    total = jnp.sum(jnp.sum(cells, axis=0), axis=0, keepdims=True)
    return sum(total[:, at : at + 128] for at in range(0, total.shape[1], 128))


def main_kernel(
    count, rows, cells, fused, source_ref, lat_ref, basis_hbm, weight_ref,
    out_ref, coef_ref,
    wide, coefs, state, halo, edge, gathered, perm, basis_ref,
    halo_send, halo_recv, sum_send, sum_recv, load_sem, *more,
):
    kept, tile, levels, lats = basis_ref.shape
    steps = coefs.shape[0]
    quads = tile // 4
    me = lax.axis_index("lon")
    west = lax.rem(me + count - 1, count)
    east = lax.rem(me + 1, count)
    barrier = pltpu.get_barrier_semaphore()

    @pl.loop(1, count)
    def _(d):
        pl.semaphore_signal(
            barrier, inc=1, device_id={"lon": lax.rem(me + d, count)},
            device_id_type=pl.DeviceIdType.MESH,
        )

    load_last = pltpu.make_async_copy(
        basis_hbm.at[kept - 1], basis_ref.at[kept - 1], load_sem.at[0]
    )
    load_rest = pltpu.make_async_copy(
        basis_hbm.at[0 : kept - 1], basis_ref.at[0 : kept - 1], load_sem.at[1]
    )
    level = lax.broadcasted_iota(jnp.int32, (levels, lats), 0)
    lat = lax.broadcasted_iota(jnp.int32, (levels, lats), 1)
    up = (level < levels - 1).astype(F32)
    down = (level > 0).astype(F32)
    not_north = (lat < lats - 1).astype(F32)
    not_south = (lat > 0).astype(F32)

    def fields(s):
        for quad in range(quads):
            at = (s * quads + quad) * rows
            block = wide[:, at : at + rows, :].reshape(lats, 128).astype(BF16)
            raw = lax.dot_general(
                block, perm[...], (((0,), (0,)), ((), ())), preferred_element_type=F32
            ).reshape(4, 4, levels, lats)
            u = 0.1 * jnp.tanh(raw[:, 0])
            v = 0.1 * jnp.tanh(raw[:, 1])
            k = 0.095 + 0.055 * jnp.tanh(0.5 * raw[:, 2])
            m = 0.06 + 0.04 * jnp.tanh(0.5 * raw[:, 3])
            cols = slice(4 * quad, 4 * quad + 4)
            coefs[s, 0, cols] = 1.0 - 4.0 * k - 2.0 * m
            coefs[s, 1, cols] = k - u
            coefs[s, 2, cols] = k + u
            coefs[s, 3, cols] = (k - v) * not_north
            coefs[s, 4, cols] = (k + v) * not_south
            coefs[s, 5, cols] = m

    def copies(slot):
        return [
            pltpu.make_async_remote_copy(
                src_ref=edge.at[slot, side],
                dst_ref=halo.at[slot, side],
                send_sem=halo_send.at[slot, side],
                recv_sem=halo_recv.at[slot, side],
                device_id={"lon": peer},
                device_id_type=pl.DeviceIdType.MESH,
            )
            for side, peer in ((0, west), (1, east))
        ]

    def send(slot, first, last):
        edge[slot, 0] = first
        edge[slot, 1] = last
        for copy in copies(slot):
            copy.start()

    def receive(slot):
        for copy in copies(slot):
            copy.wait_recv()
        return halo[slot, 0][None], halo[slot, 1][None]

    def roll(x, by, axis):
        shape = x.shape
        if axis == 2:
            return pltpu.roll(x.reshape(-1, lats), by % lats, 1).reshape(shape)
        return pltpu.roll(x, by % levels, 1)

    def forward(s, lo, hi, x, xe, xw):
        c = lambda at: coefs[s, at, lo:hi]
        return (
            c(0) * x
            + c(1) * xe
            + c(2) * xw
            + c(3) * roll(x, -1, 2)
            + c(4) * roll(x, 1, 2)
            + c(5) * (up * roll(x, -1, 1) + down * roll(x, 1, 1))
        )

    def adjoint(s, lo, hi, y, fe, fw):
        c = lambda at: coefs[s, at, lo:hi]
        d = c(5) * y
        return (
            c(0) * y
            + fe
            + fw
            + roll(c(4) * y, -1, 2)
            + roll(c(3) * y, 1, 2)
            + roll(down * d, -1, 1)
            + roll(up * d, 1, 1)
        )

    def prepare():
        perm[...] = jnp.transpose(
            (lax.broadcasted_iota(jnp.int32, (lats, lats), 0) == lat_ref[...].reshape(1, lats)).astype(F32)
        ).astype(BF16)
        gathered[me] = jnp.zeros((16, 128), F32)
        for at, (a, b) in enumerate(pairs(kept)):
            gathered[me, kept + 1 + at : kept + 2 + at, :] = row_sum(basis_ref[a] * basis_ref[b])

    def start_state():
        load_last.wait()
        state[0] = basis_ref[kept - 1]
        send(0, state[0, 0], state[0, tile - 1])

    if fused:
        raw_ref, turned, outbox, inbox, raw_sem, box_send, box_recv = more
        lanes, lons = raw_ref.shape[2], raw_ref.shape[3]
        per_step = quads * rows
        bounds = [-(-s * per_step // 16) * 16 for s in range(steps + 1)]
        loads = [
            pltpu.make_async_copy(
                source_ref.at[:, s * lanes : (s + 1) * lanes], raw_ref.at[s], raw_sem.at[s]
            )
            for s in range(steps)
        ]
        loads[0].start()
        load_last.start()
        for load in loads[1:]:
            load.start()
        load_rest.start()
        row = lax.broadcasted_iota(jnp.int32, (4 * lanes, lons), 0)
        lon = lax.broadcasted_iota(jnp.int32, (4 * lanes, lons), 1)
        quarter = lon & 3
        keep = sum(
            ((row >= lanes * q) & (row < lanes * (q + 1)) & (quarter == q)).astype(F32)
            for q in range(4)
        ).astype(BF16)
        row = lax.broadcasted_iota(jnp.int32, (lons // 4, lons), 0)
        lon = lax.broadcasted_iota(jnp.int32, (lons // 4, lons), 1)
        pick = ((lon >= 4 * row) & (lon < 4 * row + 4)).astype(F32).astype(BF16)

        def turn(s, lo, hi):
            for r in range(lo, hi):
                a = raw_ref[s, r]
                a = jnp.concatenate([a, a, a, a], axis=0) * keep
                turned[pl.ds(s * count * per_step + r, lons // 4, stride=rows), :] = (
                    lax.dot_general(
                        pick, a, (((1,), (1,)), ((), ())), preferred_element_type=F32
                    )
                )

        def step_rows(s, lo, hi):
            whole = turned[s * count * per_step : (s + 1) * count * per_step]
            return whole.reshape(count, per_step, 128)[:, lo:hi]

        def pack(p):
            lo, hi = bounds[p], bounds[p + 1]
            parts = [step_rows(p, lo - p * per_step, per_step)]
            if hi > (p + 1) * per_step:
                parts.append(step_rows(p + 1, 0, hi - (p + 1) * per_step))
            outbox[:, lo:hi] = jnp.concatenate(parts, axis=1).astype(BF16)
            inbox[me, lo:hi] = outbox[me, lo:hi]

        def box(p, target, source, d):
            lo, hi = bounds[p], bounds[p + 1]
            return pltpu.make_async_remote_copy(
                src_ref=outbox.at[target, lo:hi],
                dst_ref=inbox.at[source, lo:hi],
                send_sem=box_send.at[p, d],
                recv_sem=box_recv.at[p, source],
                device_id={"lon": target},
                device_id_type=pl.DeviceIdType.MESH,
            )

        def post(p):
            @pl.loop(1, count)
            def _(d):
                box(p, lax.rem(me + d, count), me, d).start()

        def arrive(p):
            @pl.loop(1, count)
            def _(d):
                source = lax.rem(me + d, count)
                box(p, source, source, d).wait_recv()

            lo, hi = bounds[p], bounds[p + 1]
            wide[:, lo:hi] = inbox[:, lo:hi].astype(F32)

        loads[0].wait()
        turn(0, 0, rows)
        loads[1].wait()
        turn(1, 0, 8)
        pack(0)
        pl.semaphore_wait(barrier, count - 1)
        start_state()
        post(0)
        turn(1, 8, rows)
        pack(1)
        post(1)
        for s in range(2, steps):
            loads[s].wait()
            turn(s, 0, rows)
        for s in range(2, steps):
            pack(s)
        load_rest.wait()
        prepare()
    else:
        load_last.start()
        load_rest.start()
        wide[...] = source_ref[...].astype(F32)
        pl.semaphore_wait(barrier, count - 1)
        start_state()
        load_rest.wait()
        prepare()

    flux_slot = lambda k: steps + 3 * k
    part_slot = lambda k: steps + 3 * k + 1
    coef_slot = lambda k: steps + 3 * k + 2

    for t in range(steps):
        now, new = t % 2, (t + 1) % 2
        if fused:
            arrive(t)
        fields(t)
        inside = forward(
            t, 1, tile - 1, state[now, 1 : tile - 1],
            state[now, 2:tile], state[now, 0 : tile - 2],
        )
        he, hw = receive(t)
        first = forward(t, 0, 1, state[now, 0:1], state[now, 1:2], hw)
        last = forward(
            t, tile - 1, tile, state[now, tile - 1 : tile], he,
            state[now, tile - 2 : tile - 1],
        )
        if t == steps - 1:
            inside = weight_ref[...] * inside
            first = weight_ref[...] * first
            last = weight_ref[...] * last
        else:
            send(t + 1, first[0], last[0])
        state[new, 0:1] = first
        state[new, tile - 1 : tile] = last
        state[new, 1 : tile - 1] = inside
        if t % 2 == 0:
            send(coef_slot((steps - 2 - t) // 2), coefs[t, 2, 0], coefs[t, 1, tile - 1])
        if fused and t + 2 < steps:
            post(t + 2)

    none = jnp.zeros((1, levels, lats), F32)
    for k in range(steps // 2):
        s = steps - 1 - 2 * k
        to_west = coefs[s, 2, 0:1] * state[0, 0:1]
        to_east = coefs[s, 1, tile - 1 : tile] * state[0, tile - 1 : tile]
        first = adjoint(s, 0, 1, state[0, 0:1], coefs[s, 2, 1:2] * state[0, 1:2], none)
        last = adjoint(
            s, tile - 1, tile, state[0, tile - 1 : tile], none,
            coefs[s, 1, tile - 2 : tile - 1] * state[0, tile - 2 : tile - 1],
        )
        send(flux_slot(k), to_west[0], to_east[0])
        send(part_slot(k), first[0], last[0])
        state[1, 1 : tile - 1] = adjoint(
            s, 1, tile - 1, state[0, 1 : tile - 1],
            coefs[s, 2, 2:tile] * state[0, 2:tile],
            coefs[s, 1, 0 : tile - 2] * state[0, 0 : tile - 2],
        )
        ce, cw = receive(coef_slot(k))
        he, hw = receive(flux_slot(k))
        pe, pw = receive(part_slot(k))
        state[1, 0:1] = first + hw
        state[1, tile - 1 : tile] = last + he
        he = ce * (pe + to_east)
        hw = cw * (pw + to_west)
        s = s - 1
        y = state[1]
        fe = jnp.concatenate([coefs[s, 2, 1:tile] * y[1:tile], he], axis=0)
        fw = jnp.concatenate([hw, coefs[s, 1, 0 : tile - 1] * y[0 : tile - 1]], axis=0)
        state[0] = adjoint(s, 0, tile, y, fe, fw)

    w = state[0]
    own = [row_sum(basis_ref[k] * w) for k in range(kept)] + [row_sum(w * w)]
    for k in range(kept + 1):
        gathered[me, k : k + 1, :] = own[k]

    def share(d):
        return pltpu.make_async_remote_copy(
            src_ref=gathered.at[me],
            dst_ref=gathered.at[me],
            send_sem=sum_send.at[d],
            recv_sem=sum_recv.at[me],
            device_id={"lon": lax.rem(me + d, count)},
            device_id_type=pl.DeviceIdType.MESH,
        )

    @pl.loop(1, count)
    def _(d):
        share(d).start()

    @pl.loop(1, count)
    def _(d):
        source = lax.rem(me + d, count)
        pltpu.make_async_remote_copy(
            src_ref=gathered.at[source],
            dst_ref=gathered.at[source],
            send_sem=sum_send.at[d],
            recv_sem=sum_recv.at[source],
            device_id={"lon": source},
            device_id_type=pl.DeviceIdType.MESH,
        ).wait_recv()

    total = jnp.sum(jnp.sum(gathered[...], axis=0), axis=1, keepdims=True) / cells
    c = [total[k : k + 1] for k in range(kept)]
    square = total[kept : kept + 1] - 2.0 * sum(x * x for x in c)
    for at, (a, b) in enumerate(pairs(kept)):
        g = total[kept + 1 + at : kept + 2 + at]
        square = square + (1.0 if a == b else 2.0) * c[a] * c[b] * g
    beta = jnp.sqrt(square + 1e-06)
    lane = lax.broadcasted_iota(jnp.int32, (8, 128), 1)
    coef_ref[...] = sum(
        jnp.where(lane == k, jnp.broadcast_to(x, (8, 128)), 0.0)
        for k, x in enumerate(c + [beta])
    )
    scale = jnp.broadcast_to(1.0 / beta, (levels, lats))
    full = [jnp.broadcast_to(x, (levels, lats)) for x in c]
    for i in range(tile):
        r = state[0, i]
        for k in range(kept):
            r = r - full[k] * basis_ref[k, i]
        out_ref[i] = r * scale

    for t in range(steps + 3 * (steps // 2)):
        for copy in copies(t):
            copy.wait_send()

    @pl.loop(1, count)
    def _(d):
        share(d).wait_send()

    if fused:
        for p in range(steps):

            @pl.loop(1, count)
            def _(d, p=p):
                box(p, lax.rem(me + d, count), me, d).wait_send()


def shards(trajectory, lat_order, basis, weight):
    rows, steps, states, levels, lons = trajectory.shape
    kept, _, tile, lats = basis.shape
    count = lax.axis_size("lon")
    lanes = steps * states * levels
    cells = float(levels * lons * lats)
    flat = trajectory.reshape(rows, lanes, lons)
    quads = tile // 4
    fused = rows % 8 == 0 and (steps * quads * rows) % 16 == 0 and steps % 2 == 0
    slots = steps + 3 * (steps // 2)
    more = []
    if fused:
        source, place, blocks, run = flat, pl.BlockSpec(memory_space=pl.ANY), count, rows
        more = [
            pltpu.VMEM((steps, rows, lanes // steps, lons), BF16),
            pltpu.VMEM((lons * rows, lanes), F32),
            pltpu.VMEM((count, tile * rows, lanes), BF16),
            pltpu.VMEM((count, tile * rows, lanes), BF16),
            pltpu.SemaphoreType.DMA((steps,)),
            pltpu.SemaphoreType.DMA((steps, count)),
            pltpu.SemaphoreType.DMA((steps, count)),
        ]
    else:
        packed = jnp.transpose(flat, (2, 0, 1)).reshape(count, tile * rows, lanes)
        got = lax.all_to_all(packed, "lon", split_axis=0, concat_axis=0, tiled=True)
        got = got.reshape(count, quads, 4, rows, steps, lanes // steps)
        got = jnp.transpose(got, (4, 1, 0, 3, 2, 5))
        source, place, blocks, run = got.reshape(1, tile * lats, lanes), VMEM, 1, lats
    out, coef = pl.pallas_call(
        functools.partial(main_kernel, count, run, cells, fused),
        out_shape=(
            jax.ShapeDtypeStruct((tile, levels, lats), F32),
            jax.ShapeDtypeStruct((8, 128), F32),
        ),
        in_specs=[place, VMEM, pl.BlockSpec(memory_space=pl.ANY), VMEM],
        out_specs=(VMEM, VMEM),
        scratch_shapes=[
            pltpu.VMEM((blocks, tile * run, lanes), F32),
            pltpu.VMEM((steps, 6, tile, levels, lats), F32),
            pltpu.VMEM((2, tile, levels, lats), F32),
            pltpu.VMEM((slots, 2, levels, lats), F32),
            pltpu.VMEM((slots, 2, levels, lats), F32),
            pltpu.VMEM((count, 16, 128), F32),
            pltpu.VMEM((lats, lats), BF16),
            pltpu.VMEM((kept, tile, levels, lats), F32),
            pltpu.SemaphoreType.DMA((slots, 2)),
            pltpu.SemaphoreType.DMA((slots, 2)),
            pltpu.SemaphoreType.DMA((count,)),
            pltpu.SemaphoreType.DMA((count,)),
            pltpu.SemaphoreType.DMA((2,)),
        ]
        + more,
        compiler_params=pltpu.CompilerParams(
            collective_id=0, has_side_effects=True, vmem_limit_bytes=63 * MIB
        ),
        name="iterate",
    )(source, lat_order, jnp.transpose(basis, (0, 2, 1, 3)), weight)
    return jnp.transpose(out, (1, 0, 2)), coef[0, : kept + 1]


def solution(mesh):
    placed = (P(("grp", "lon"), None, None, None, None), P(), P("grp", None, "lon", None), P())
    return jax.shard_map(
        shards,
        mesh=mesh,
        in_specs=placed,
        out_specs=(P("grp", "lon", None), P("grp")),
        check_vma=False,
    )
```

```python
import functools

import jax
import jax.numpy as jnp
from jax import lax
from jax.experimental import pallas as pl
from jax.experimental.pallas import tpu as pltpu
from jax.sharding import PartitionSpec as P

BF16 = jnp.bfloat16
F32 = jnp.float32
VMEM = pl.BlockSpec(memory_space=pltpu.VMEM)
MIB = 1024 * 1024


def pairs(kept):
    return [(a, b) for a in range(kept) for b in range(a, kept)]


def row_sum(cells):
    total = jnp.sum(jnp.sum(cells, axis=0), axis=0, keepdims=True)
    return sum(total[:, at : at + 128] for at in range(0, total.shape[1], 128))


def main_kernel(
    count, rows, cells, fused, source_ref, lat_ref, basis_hbm, weight_ref,
    out_ref, coef_ref,
    wide, coefs, state, halo, edge, gathered, perm, basis_ref,
    halo_send, halo_recv, sum_send, sum_recv, load_sem, *more,
):
    kept, tile, levels, lats = basis_ref.shape
    steps = coefs.shape[0]
    quads = tile // 4
    me = lax.axis_index("lon")
    west = lax.rem(me + count - 1, count)
    east = lax.rem(me + 1, count)
    barrier = pltpu.get_barrier_semaphore()

    @pl.loop(1, count)
    def _(d):
        pl.semaphore_signal(
            barrier, inc=1, device_id={"lon": lax.rem(me + d, count)},
            device_id_type=pl.DeviceIdType.MESH,
        )

    load_last = pltpu.make_async_copy(
        basis_hbm.at[kept - 1], basis_ref.at[kept - 1], load_sem.at[0]
    )
    load_rest = pltpu.make_async_copy(
        basis_hbm.at[0 : kept - 1], basis_ref.at[0 : kept - 1], load_sem.at[1]
    )
    level = lax.broadcasted_iota(jnp.int32, (levels, lats), 0)
    lat = lax.broadcasted_iota(jnp.int32, (levels, lats), 1)
    up = (level < levels - 1).astype(F32)
    down = (level > 0).astype(F32)
    not_north = (lat < lats - 1).astype(F32)
    not_south = (lat > 0).astype(F32)

    def fields(s):
        for quad in range(quads):
            at = (s * quads + quad) * rows
            block = wide[:, at : at + rows, :].reshape(lats, 128).astype(BF16)
            raw = lax.dot_general(
                block, perm[...], (((0,), (0,)), ((), ())), preferred_element_type=F32
            ).reshape(4, 4, levels, lats)
            u = 0.1 * jnp.tanh(raw[:, 0])
            v = 0.1 * jnp.tanh(raw[:, 1])
            k = 0.095 + 0.055 * jnp.tanh(0.5 * raw[:, 2])
            m = 0.06 + 0.04 * jnp.tanh(0.5 * raw[:, 3])
            cols = slice(4 * quad, 4 * quad + 4)
            coefs[s, 0, cols] = 1.0 - 4.0 * k - 2.0 * m
            coefs[s, 1, cols] = k - u
            coefs[s, 2, cols] = k + u
            coefs[s, 3, cols] = (k - v) * not_north
            coefs[s, 4, cols] = (k + v) * not_south
            coefs[s, 5, cols] = m

    def copies(slot):
        return [
            pltpu.make_async_remote_copy(
                src_ref=edge.at[slot, side],
                dst_ref=halo.at[slot, side],
                send_sem=halo_send.at[slot, side],
                recv_sem=halo_recv.at[slot, side],
                device_id={"lon": peer},
                device_id_type=pl.DeviceIdType.MESH,
            )
            for side, peer in ((0, west), (1, east))
        ]

    def send(slot, first, last):
        edge[slot, 0] = first
        edge[slot, 1] = last
        for copy in copies(slot):
            copy.start()

    def receive(slot):
        for copy in copies(slot):
            copy.wait_recv()
        return halo[slot, 0][None], halo[slot, 1][None]

    def roll(x, by, axis):
        shape = x.shape
        if axis == 2:
            return pltpu.roll(x.reshape(-1, lats), by % lats, 1).reshape(shape)
        return pltpu.roll(x, by % levels, 1)

    def forward(s, lo, hi, x, xe, xw):
        c = lambda at: coefs[s, at, lo:hi]
        return (
            c(0) * x
            + c(1) * xe
            + c(2) * xw
            + c(3) * roll(x, -1, 2)
            + c(4) * roll(x, 1, 2)
            + c(5) * (up * roll(x, -1, 1) + down * roll(x, 1, 1))
        )

    def adjoint(s, lo, hi, y, fe, fw):
        c = lambda at: coefs[s, at, lo:hi]
        d = c(5) * y
        return (
            c(0) * y
            + fe
            + fw
            + roll(c(4) * y, -1, 2)
            + roll(c(3) * y, 1, 2)
            + roll(down * d, -1, 1)
            + roll(up * d, 1, 1)
        )

    def prepare():
        perm[...] = jnp.transpose(
            (lax.broadcasted_iota(jnp.int32, (lats, lats), 0) == lat_ref[...].reshape(1, lats)).astype(F32)
        ).astype(BF16)
        gathered[me] = jnp.zeros((16, 128), F32)
        for at, (a, b) in enumerate(pairs(kept)):
            gathered[me, kept + 1 + at : kept + 2 + at, :] = row_sum(basis_ref[a] * basis_ref[b])

    def start_state():
        load_last.wait()
        state[0] = basis_ref[kept - 1]
        send(0, state[0, 0], state[0, tile - 1])

    if fused:
        raw_ref, turned, outbox, inbox, raw_sem, box_send, box_recv = more
        lanes, lons = raw_ref.shape[2], raw_ref.shape[3]
        per_step = quads * rows
        bounds = [-(-s * per_step // 16) * 16 for s in range(steps + 1)]
        loads = [
            pltpu.make_async_copy(
                source_ref.at[:, s * lanes : (s + 1) * lanes], raw_ref.at[s], raw_sem.at[s]
            )
            for s in range(steps)
        ]
        loads[0].start()
        load_last.start()
        for load in loads[1:]:
            load.start()
        load_rest.start()
        row = lax.broadcasted_iota(jnp.int32, (4 * lanes, lons), 0)
        lon = lax.broadcasted_iota(jnp.int32, (4 * lanes, lons), 1)
        quarter = lon & 3
        keep = sum(
            ((row >= lanes * q) & (row < lanes * (q + 1)) & (quarter == q)).astype(F32)
            for q in range(4)
        ).astype(BF16)
        row = lax.broadcasted_iota(jnp.int32, (lons // 4, lons), 0)
        lon = lax.broadcasted_iota(jnp.int32, (lons // 4, lons), 1)
        pick = ((lon >= 4 * row) & (lon < 4 * row + 4)).astype(F32).astype(BF16)

        def turn(s, lo, hi):
            for r in range(lo, hi):
                a = raw_ref[s, r]
                a = jnp.concatenate([a, a, a, a], axis=0) * keep
                turned[pl.ds(s * count * per_step + r, lons // 4, stride=rows), :] = (
                    lax.dot_general(
                        pick, a, (((1,), (1,)), ((), ())), preferred_element_type=F32
                    )
                )

        def step_rows(s, lo, hi):
            whole = turned[s * count * per_step : (s + 1) * count * per_step]
            return whole.reshape(count, per_step, 128)[:, lo:hi]

        def pack(p):
            lo, hi = bounds[p], bounds[p + 1]
            parts = [step_rows(p, lo - p * per_step, per_step)]
            if hi > (p + 1) * per_step:
                parts.append(step_rows(p + 1, 0, hi - (p + 1) * per_step))
            outbox[:, lo:hi] = jnp.concatenate(parts, axis=1).astype(BF16)
            inbox[me, lo:hi] = outbox[me, lo:hi]

        def box(p, target, source, d):
            lo, hi = bounds[p], bounds[p + 1]
            return pltpu.make_async_remote_copy(
                src_ref=outbox.at[target, lo:hi],
                dst_ref=inbox.at[source, lo:hi],
                send_sem=box_send.at[p, d],
                recv_sem=box_recv.at[p, source],
                device_id={"lon": target},
                device_id_type=pl.DeviceIdType.MESH,
            )

        def post(p):
            @pl.loop(1, count)
            def _(d):
                at = lax.rem(d + count // 2 - 2, count - 1) + 1
                box(p, lax.rem(me + at, count), me, at).start()

        def arrive(p):
            @pl.loop(1, count)
            def _(d):
                source = lax.rem(me + d, count)
                box(p, source, source, d).wait_recv()

            lo, hi = bounds[p], bounds[p + 1]
            wide[:, lo:hi] = inbox[:, lo:hi].astype(F32)

        loads[0].wait()
        turn(0, 0, rows)
        loads[1].wait()
        turn(1, 0, 8)
        pack(0)
        pl.semaphore_wait(barrier, count - 1)
        start_state()
        post(0)
        turn(1, 8, rows)
        pack(1)
        post(1)
        for s in range(2, steps):
            loads[s].wait()
            turn(s, 0, rows)
        for s in range(2, steps):
            pack(s)
        load_rest.wait()
        prepare()
    else:
        load_last.start()
        load_rest.start()
        wide[...] = source_ref[...].astype(F32)
        pl.semaphore_wait(barrier, count - 1)
        start_state()
        load_rest.wait()
        prepare()

    flux_slot = lambda k: steps + 3 * k
    part_slot = lambda k: steps + 3 * k + 1
    coef_slot = lambda k: steps + 3 * k + 2

    for t in range(steps):
        now, new = t % 2, (t + 1) % 2
        if fused:
            arrive(t)
        fields(t)
        inside = forward(
            t, 1, tile - 1, state[now, 1 : tile - 1],
            state[now, 2:tile], state[now, 0 : tile - 2],
        )
        he, hw = receive(t)
        first = forward(t, 0, 1, state[now, 0:1], state[now, 1:2], hw)
        last = forward(
            t, tile - 1, tile, state[now, tile - 1 : tile], he,
            state[now, tile - 2 : tile - 1],
        )
        if t == steps - 1:
            inside = weight_ref[...] * inside
            first = weight_ref[...] * first
            last = weight_ref[...] * last
        else:
            send(t + 1, first[0], last[0])
        state[new, 0:1] = first
        state[new, tile - 1 : tile] = last
        state[new, 1 : tile - 1] = inside
        if t % 2 == 0:
            send(coef_slot((steps - 2 - t) // 2), coefs[t, 2, 0], coefs[t, 1, tile - 1])
        if fused and t + 2 < steps:
            post(t + 2)

    none = jnp.zeros((1, levels, lats), F32)
    for k in range(steps // 2):
        s = steps - 1 - 2 * k
        to_west = coefs[s, 2, 0:1] * state[0, 0:1]
        to_east = coefs[s, 1, tile - 1 : tile] * state[0, tile - 1 : tile]
        first = adjoint(s, 0, 1, state[0, 0:1], coefs[s, 2, 1:2] * state[0, 1:2], none)
        last = adjoint(
            s, tile - 1, tile, state[0, tile - 1 : tile], none,
            coefs[s, 1, tile - 2 : tile - 1] * state[0, tile - 2 : tile - 1],
        )
        send(flux_slot(k), to_west[0], to_east[0])
        send(part_slot(k), first[0], last[0])
        state[1, 1 : tile - 1] = adjoint(
            s, 1, tile - 1, state[0, 1 : tile - 1],
            coefs[s, 2, 2:tile] * state[0, 2:tile],
            coefs[s, 1, 0 : tile - 2] * state[0, 0 : tile - 2],
        )
        ce, cw = receive(coef_slot(k))
        he, hw = receive(flux_slot(k))
        pe, pw = receive(part_slot(k))
        state[1, 0:1] = first + hw
        state[1, tile - 1 : tile] = last + he
        he = ce * (pe + to_east)
        hw = cw * (pw + to_west)
        s = s - 1
        y = state[1]
        fe = jnp.concatenate([coefs[s, 2, 1:tile] * y[1:tile], he], axis=0)
        fw = jnp.concatenate([hw, coefs[s, 1, 0 : tile - 1] * y[0 : tile - 1]], axis=0)
        state[0] = adjoint(s, 0, tile, y, fe, fw)

    w = state[0]
    own = [row_sum(basis_ref[k] * w) for k in range(kept)] + [row_sum(w * w)]
    for k in range(kept + 1):
        gathered[me, k : k + 1, :] = own[k]

    def share(d):
        return pltpu.make_async_remote_copy(
            src_ref=gathered.at[me],
            dst_ref=gathered.at[me],
            send_sem=sum_send.at[d],
            recv_sem=sum_recv.at[me],
            device_id={"lon": lax.rem(me + d, count)},
            device_id_type=pl.DeviceIdType.MESH,
        )

    @pl.loop(1, count)
    def _(d):
        share(d).start()

    @pl.loop(1, count)
    def _(d):
        source = lax.rem(me + d, count)
        pltpu.make_async_remote_copy(
            src_ref=gathered.at[source],
            dst_ref=gathered.at[source],
            send_sem=sum_send.at[d],
            recv_sem=sum_recv.at[source],
            device_id={"lon": source},
            device_id_type=pl.DeviceIdType.MESH,
        ).wait_recv()

    total = jnp.sum(jnp.sum(gathered[...], axis=0), axis=1, keepdims=True) / cells
    c = [total[k : k + 1] for k in range(kept)]
    square = total[kept : kept + 1] - 2.0 * sum(x * x for x in c)
    for at, (a, b) in enumerate(pairs(kept)):
        g = total[kept + 1 + at : kept + 2 + at]
        square = square + (1.0 if a == b else 2.0) * c[a] * c[b] * g
    beta = jnp.sqrt(square + 1e-06)
    lane = lax.broadcasted_iota(jnp.int32, (8, 128), 1)
    coef_ref[...] = sum(
        jnp.where(lane == k, jnp.broadcast_to(x, (8, 128)), 0.0)
        for k, x in enumerate(c + [beta])
    )
    scale = jnp.broadcast_to(1.0 / beta, (levels, lats))
    full = [jnp.broadcast_to(x, (levels, lats)) for x in c]
    for i in range(tile):
        r = state[0, i]
        for k in range(kept):
            r = r - full[k] * basis_ref[k, i]
        out_ref[i] = r * scale

    for t in range(steps + 3 * (steps // 2)):
        for copy in copies(t):
            copy.wait_send()

    @pl.loop(1, count)
    def _(d):
        share(d).wait_send()

    if fused:
        for p in range(steps):

            @pl.loop(1, count)
            def _(d, p=p):
                box(p, lax.rem(me + d, count), me, d).wait_send()


def shards(trajectory, lat_order, basis, weight):
    rows, steps, states, levels, lons = trajectory.shape
    kept, _, tile, lats = basis.shape
    count = lax.axis_size("lon")
    lanes = steps * states * levels
    cells = float(levels * lons * lats)
    flat = trajectory.reshape(rows, lanes, lons)
    quads = tile // 4
    fused = rows % 8 == 0 and (steps * quads * rows) % 16 == 0 and steps % 2 == 0
    slots = steps + 3 * (steps // 2)
    more = []
    if fused:
        source, place, blocks, run = flat, pl.BlockSpec(memory_space=pl.ANY), count, rows
        more = [
            pltpu.VMEM((steps, rows, lanes // steps, lons), BF16),
            pltpu.VMEM((lons * rows, lanes), F32),
            pltpu.VMEM((count, tile * rows, lanes), BF16),
            pltpu.VMEM((count, tile * rows, lanes), BF16),
            pltpu.SemaphoreType.DMA((steps,)),
            pltpu.SemaphoreType.DMA((steps, count)),
            pltpu.SemaphoreType.DMA((steps, count)),
        ]
    else:
        packed = jnp.transpose(flat, (2, 0, 1)).reshape(count, tile * rows, lanes)
        got = lax.all_to_all(packed, "lon", split_axis=0, concat_axis=0, tiled=True)
        got = got.reshape(count, quads, 4, rows, steps, lanes // steps)
        got = jnp.transpose(got, (4, 1, 0, 3, 2, 5))
        source, place, blocks, run = got.reshape(1, tile * lats, lanes), VMEM, 1, lats
    out, coef = pl.pallas_call(
        functools.partial(main_kernel, count, run, cells, fused),
        out_shape=(
            jax.ShapeDtypeStruct((tile, levels, lats), F32),
            jax.ShapeDtypeStruct((8, 128), F32),
        ),
        in_specs=[place, VMEM, pl.BlockSpec(memory_space=pl.ANY), VMEM],
        out_specs=(VMEM, VMEM),
        scratch_shapes=[
            pltpu.VMEM((blocks, tile * run, lanes), F32),
            pltpu.VMEM((steps, 6, tile, levels, lats), F32),
            pltpu.VMEM((2, tile, levels, lats), F32),
            pltpu.VMEM((slots, 2, levels, lats), F32),
            pltpu.VMEM((slots, 2, levels, lats), F32),
            pltpu.VMEM((count, 16, 128), F32),
            pltpu.VMEM((lats, lats), BF16),
            pltpu.VMEM((kept, tile, levels, lats), F32),
            pltpu.SemaphoreType.DMA((slots, 2)),
            pltpu.SemaphoreType.DMA((slots, 2)),
            pltpu.SemaphoreType.DMA((count,)),
            pltpu.SemaphoreType.DMA((count,)),
            pltpu.SemaphoreType.DMA((2,)),
        ]
        + more,
        compiler_params=pltpu.CompilerParams(
            collective_id=0, has_side_effects=True, vmem_limit_bytes=63 * MIB
        ),
        name="iterate",
    )(source, lat_order, jnp.transpose(basis, (0, 2, 1, 3)), weight)
    return jnp.transpose(out, (1, 0, 2)), coef[0, : kept + 1]


def solution(mesh):
    placed = (P(("grp", "lon"), None, None, None, None), P(), P("grp", None, "lon", None), P())
    return jax.shard_map(
        shards,
        mesh=mesh,
        in_specs=placed,
        out_specs=(P("grp", "lon", None), P("grp")),
        check_vma=False,
    )
```
